32 devices in a mesh: front: 2 (over x), row: 4 (over z), col: 4 (over y, core).
Axes of the slice: x: 2, y: 2, z: 4, core: 2. Of those that a mesh axis runs over, the one named last changes fastest.
Arguments:
- child_blocks: float32 [2, 4, 4, 2, 8, 128, 128], P('front', 'row', 'col'), may hold values from -0.15232572 to 0.15232572
- child_map: int32 [2, 4, 4, 2, 8], P('front', 'row', 'col'), may hold values from 0 to 63, as said below
- stiff_diag: float32 [2, 4096], P('front'), may hold values from 2.5 to 4
- pivot_blocks: int32 [2], P('front'), may hold values from 1 to 4, as said below
Outputs:
- factored: float32 [2, 4, 8, 128, 4, 8, 128], P('front', 'row', None, None, 'col')
The draws below stay inside these ranges and needn't reach their ends.
Inputs may be any that keep to these rules, and one draw needn't show every extreme that they name: `child_map`: each entry t names a block (t // (F / 512), t % (F / 512)) of the receiving device r, c whose global block row r + 4 (t // (F / 512)) is not below its global block column c + 4 (t % (F / 512)). `pivot_blocks`: exactly one front has 4; every other front has fewer.
All inputs are finite; a program needn't handle non-finite values.
Results may differ from the reference program's by a relative error of at most 0.0003.
Values sent between devices are 32-bit elements; how exact they have to be, the bound alone decides.
A program may use at most 128 MiB of HBM per device.

```python
import jax
import jax.numpy as jnp
from jax import lax

BS = 128
F = 4096
NP = 4
SLOTS = 8
N_FRONT = 2
N_ROW = 4
N_COL = 4


def draw_pivot_blocks(key, part):
    first_key, second_key = jax.random.split(jax.random.fold_in(key, 31))
    counts = jax.random.randint(first_key, (N_FRONT,), 1, NP)
    chosen = jax.random.randint(second_key, (), 0, N_FRONT)
    return jnp.where(jnp.arange(N_FRONT) == chosen, NP, counts).astype(jnp.int32)


def draw_child_map(key, part):
    down_count = F // (BS * N_ROW)
    across_count = F // (BS * N_COL)
    shape = (N_FRONT, N_ROW, N_COL, N_FRONT, SLOTS)
    row_place = jnp.broadcast_to(jnp.arange(N_ROW, dtype=jnp.int32).reshape(1, N_ROW, 1, 1, 1), shape)
    col_place = jnp.broadcast_to(jnp.arange(N_COL, dtype=jnp.int32).reshape(1, 1, N_COL, 1, 1), shape)
    first_key, second_key = jax.random.split(jax.random.fold_in(key, 23))
    first = jax.random.randint(first_key, shape, 0, down_count)
    second = jax.random.randint(second_key, shape, 0, down_count)
    block_down = jnp.maximum(first, second)
    block_across = jnp.minimum(first, second)
    clash = (block_down == block_across) & (row_place < col_place)
    moved_down = jnp.where(block_down >= 1, block_down, 1)
    moved_across = jnp.where(block_down >= 1, block_down - 1, 0)
    block_down = jnp.where(clash, moved_down, block_down)
    block_across = jnp.where(clash, moved_across, block_across)
    return (block_down * across_count + block_across).astype(jnp.int32)


def draw_child_blocks(key, part):
    block_total = F // BS
    spread = 0.6 * (block_total * (block_total + 1)) ** 0.5 / (2 * N_FRONT * N_ROW * N_COL * SLOTS * NP * BS) ** 0.5
    shape = (N_FRONT, N_ROW, N_COL, N_FRONT, SLOTS, BS, BS)
    own_key = jax.random.fold_in(key, 11)
    values = jnp.clip(jax.random.normal(own_key, shape, jnp.float32), -4.0, 4.0)
    return (spread * values).astype(jnp.float32)


def shard_levels(stream_key, dims, pieces, smallest, largest):
    factor_of = 1.0
    for axis_at, shards_of in pieces:
        draws = jax.random.uniform(jax.random.fold_in(jax.random.fold_in(stream_key, 6), axis_at), (shards_of,), jnp.float32, smallest / len(pieces), largest / len(pieces))
        factor_of = factor_of * jnp.repeat(jnp.exp(draws), dims[axis_at] // shards_of).reshape((-1,) + (1,) * (len(dims) - 1 - axis_at))
    return factor_of


def setup_inputs(seed: int = 0) -> dict:
    streams_of = jax.random.split(jax.random.key(seed), 5)
    return {
        "child_blocks": draw_child_blocks(jax.random.fold_in(streams_of[4], 71), 0),
        "child_map": draw_child_map(jax.random.fold_in(streams_of[4], 71), 0),
        "stiff_diag": jnp.clip(2.5 + 1.5 * jax.random.uniform(streams_of[2], (N_FRONT, F), jnp.float32) ** shard_levels(streams_of[2], (N_FRONT, F), ((0, 2),), -0.2, 0.2), 2.5, 4.0),
        "pivot_blocks": draw_pivot_blocks(jax.random.fold_in(streams_of[4], 71), 0),
    }


def front_result(front_id, child_blocks, child_map, stiff_diag, pivot_blocks):
    down_count = F // (BS * N_ROW)
    across_count = F // (BS * N_COL)
    block_total = F // BS
    blocks = lax.dynamic_index_in_dim(child_blocks, front_id, 3, keepdims=False)
    targets = lax.dynamic_index_in_dim(child_map, front_id, 0, keepdims=False)
    targets = jnp.transpose(targets, (2, 0, 1, 3))
    row_place = jnp.arange(N_ROW, dtype=jnp.int32).reshape(1, N_ROW, 1, 1)
    col_place = jnp.arange(N_COL, dtype=jnp.int32).reshape(1, 1, N_COL, 1)
    block_row = row_place + N_ROW * (targets // across_count)
    block_col = col_place + N_COL * (targets % across_count)
    segment_ids = (block_row * block_total + block_col).reshape(-1).astype(jnp.int32)
    summed = jax.ops.segment_sum(blocks.reshape(-1, BS, BS), segment_ids, num_segments=block_total * block_total)
    assembled = summed.reshape(block_total, block_total, BS, BS).transpose(0, 2, 1, 3).reshape(F, F)
    diag_vals = lax.dynamic_index_in_dim(stiff_diag, front_id, 0, keepdims=False)
    matrix = jnp.tril(assembled) + jnp.tril(assembled, -1).T + jnp.diag(diag_vals)
    panel = NP * BS
    pivot_count = lax.dynamic_index_in_dim(pivot_blocks, front_id, 0, keepdims=False) * BS
    chosen = jnp.arange(panel, dtype=jnp.int32) < pivot_count
    both = chosen[:, None] & chosen[None, :]
    leading = jnp.where(both, matrix[:panel, :panel], jnp.eye(panel, dtype=jnp.float32))
    lower_factor = jnp.linalg.cholesky(leading)
    right_part = matrix[:, :panel] * chosen[None, :].astype(jnp.float32)
    solved = lax.linalg.triangular_solve(lower_factor, right_part, left_side=False, lower=True, transpose_a=True)
    schur_part = matrix - jnp.dot(solved.astype(jnp.float32), solved.T.astype(jnp.float32), precision=lax.Precision.HIGHEST, preferred_element_type=jnp.float32)
    padded = jnp.concatenate([solved, jnp.zeros((F, F - panel), jnp.float32)], axis=1)
    columns = jnp.arange(F, dtype=jnp.int32)
    result = jnp.where(columns[None, :] < pivot_count, padded, schur_part)
    result = jnp.tril(result)
    return result.reshape(down_count, N_ROW, BS, across_count, N_COL, BS).transpose(1, 0, 2, 4, 3, 5)

def reference(child_blocks, child_map, stiff_diag, pivot_blocks):

    def one_front(front_id):
        return front_result(front_id, child_blocks, child_map, stiff_diag, pivot_blocks)
    return lax.map(one_front, jnp.arange(N_FRONT, dtype=jnp.int32))
```

```python
import functools

import jax
import jax.numpy as jnp
from jax import lax
from jax.experimental import pallas as pl
from jax.experimental.pallas import tpu as pltpu
from jax.sharding import PartitionSpec as P

NP = 4
GROUP = 4
NT = (((1,), (1,)), ((), ()))
TN = (((0,), (0,)), ((), ()))
NN = (((1,), (0,)), ((), ()))
F32 = jnp.float32
BF16 = jnp.bfloat16
VMEM_BYTES = 44 * 1024 * 1024


def exact_dot(a, b, dims):
    return lax.dot_general(
        a, b, dims, precision=lax.Precision.HIGHEST, preferred_element_type=F32
    )


def split(x):
    high = x.astype(BF16)
    return high, (x - high.astype(F32)).astype(BF16)


def split_dot(a, b, dims):
    dot = functools.partial(lax.dot_general, dimension_numbers=dims, preferred_element_type=F32)
    return dot(a[0], b[0]) + (dot(a[0], b[1]) + dot(a[1], b[0]))


def panel_kernel(slots, across, targets, blocks, out):
    out[...] = jnp.zeros_like(out)

    def body(s, carry):
        t = targets[s]

        @pl.when(lax.rem(t, across) == 0)
        def _():
            i = lax.div(t, across)
            out[i] = out[i] + blocks[s]

        return carry

    lax.fori_loop(0, slots, body, 0)


def invert_diagonal(block, bs):
    tiles = bs // 8
    sub = lax.broadcasted_iota(jnp.int32, (8, bs), 0)
    lane = lax.broadcasted_iota(jnp.int32, (8, bs), 1)
    m = [block[8 * i : 8 * i + 8, :] for i in range(tiles)]
    w = [(lane == sub + 8 * i).astype(F32) for i in range(tiles)]
    for k in range(0, bs, GROUP):
        top = k // 8
        cols = [
            {
                i: jnp.broadcast_to(m[i][:, k + t : k + t + 1], (8, bs))
                for i in range(top, tiles)
            }
            for t in range(GROUP)
        ]
        for t in range(GROUP):
            kk = k % 8 + t
            inv = 1.0 / cols[t][top][kk : kk + 1, :]
            q = m[top][kk : kk + 1, :] * inv
            wq = w[top][kk : kk + 1, :] * inv
            rest = {s: cols[s][top][kk : kk + 1, :] * inv for s in range(t + 1, GROUP)}
            for i in range(top, tiles):
                c = cols[t][i]
                if i == top:
                    if kk == 7:
                        continue
                    c = jnp.where(sub > kk, c, 0.0)
                m[i] = m[i] - c * q
                w[i] = w[i] - c * wq
                for s in rest:
                    cols[s][i] = cols[s][i] - c * rest[s]
    out = []
    for i in range(tiles):
        d = jnp.sum(jnp.where(lane == sub + 8 * i, m[i], 0.0), axis=1, keepdims=True)
        out.append(w[i] * lax.rsqrt(d))
    return jnp.concatenate(out, axis=0)


def factor_kernel(bs, scal, lead, stiff, inverse, full, work):
    n = NP * bs
    pivot = scal[2]
    row = lax.broadcasted_iota(jnp.int32, (bs, bs), 0)
    col = lax.broadcasted_iota(jnp.int32, (bs, bs), 1)
    eye = row == col
    for i in range(NP):
        for j in range(i + 1):
            block = lead[i * NP + j]
            if i == j:
                block = jnp.where(row >= col, block, block.T)
                block = block + jnp.where(eye, stiff[i : i + 1, :], 0.0)
            full[i * bs : (i + 1) * bs, j * bs : (j + 1) * bs] = block
            if i != j:
                full[j * bs : (j + 1) * bs, i * bs : (i + 1) * bs] = block.T
    for i in range(NP):
        for j in range(NP):
            ok = jnp.logical_and(i < pivot, j < pivot)
            rest = eye.astype(F32) if i == j else jnp.zeros((bs, bs), F32)
            work[i * bs : (i + 1) * bs, j * bs : (j + 1) * bs] = jnp.where(
                ok, full[i * bs : (i + 1) * bs, j * bs : (j + 1) * bs], rest
            )
            work[i * bs : (i + 1) * bs, n + j * bs : n + (j + 1) * bs] = (
                eye.astype(F32) if i == j else jnp.zeros((bs, bs), F32)
            )

    for b in range(NP):
        lo, hi = b * bs, (b + 1) * bs
        w = invert_diagonal(work[lo:hi, lo:hi], bs)
        done = exact_dot(w, work[lo:hi, lo : n + hi], NN)
        inverse[lo:hi, :] = jnp.where(b < pivot, jnp.concatenate(
            [done[:, n - lo :]] + ([jnp.zeros((bs, n - hi), F32)] if hi < n else []), axis=1
        ), 0.0)
        if hi < n:
            work[hi:, hi : n + hi] = work[hi:, hi : n + hi] - exact_dot(
                done[:, bs : n - lo], done[:, bs:], TN
            )


def update_kernel(
    slots, across, rows_n, cols_n, bs, scal, targets, blocks, row_part, col_part, full, inverse,
    stiff, out, inv_hi, inv_lo, col_hi, col_lo, total,
):
    i = pl.program_id(0)
    down = pl.num_programs(0)
    r, c, pivot = scal[0], scal[1], scal[2]

    def solved(part, k, place):
        def first():
            return full[pl.ds(pl.multiple_of(place * bs, bs), bs), :]

        a = jnp.concatenate([part[j, jnp.maximum(k - 1, 0)] for j in range(NP)], axis=1)
        a = jnp.where(k == 0, first(), a)
        return split_dot(split(a), (inv_hi[...], inv_lo[...]), NT)

    @pl.when(i == 0)
    def _():
        high, low = split(inverse[...])
        inv_hi[...] = high
        inv_lo[...] = low

    high, low = split(solved(col_part, i, c))
    at = pl.ds(pl.multiple_of(i * bs, bs), bs)
    col_hi[at, :] = high
    col_lo[at, :] = low
    x = solved(row_part, i, r)
    mine = split(x)
    total[...] = jnp.zeros_like(total)

    def body(s, carry):
        t = targets[s]

        @pl.when(lax.div(t, across) == i)
        def _():
            j = lax.rem(t, across)
            total[j] = total[j] + blocks[s]

        return carry

    lax.fori_loop(0, slots, body, 0)
    place = r + rows_n * i
    row = lax.broadcasted_iota(jnp.int32, (bs, bs), 0)
    col = lax.broadcasted_iota(jnp.int32, (bs, bs), 1)
    stiff_row = stiff[pl.ds(place, 1), :]

    for j in range(across):
        across_place = c + cols_n * j

        @pl.when(place > across_place)
        def _():
            at_j = slice(j * bs, (j + 1) * bs)
            v = total[j] - split_dot(mine, (col_hi[at_j, :], col_lo[at_j, :]), NT)
            total[j] = v

        @pl.when(place == across_place)
        def _():
            at_j = slice(j * bs, (j + 1) * bs)
            v = total[j] - split_dot(mine, (col_hi[at_j, :], col_lo[at_j, :]), NT)
            v = v + jnp.where(row == col, stiff_row, 0.0)
            total[j] = jnp.where(row >= col, v, 0.0)

        if j == 0:
            for b in range(NP):

                @pl.when((c == b) & (b < pivot))
                def _():
                    mask = (place > b) | ((place == b) & (row >= col))
                    total[0] = jnp.where(mask, x[:, b * bs : (b + 1) * bs], 0.0)

        out[0, pl.ds(j, bs, stride=across), :] = total[j]


def on_device(child_blocks, child_map, stiff_diag, pivot_blocks):
    frames, slot_count, bs = child_blocks.shape[3:6]
    rows_n, cols_n = lax.axis_size("row"), lax.axis_size("col")
    order = stiff_diag.shape[1]
    down, across = order // (bs * rows_n), order // (bs * cols_n)
    slots = frames * slot_count
    r, c = lax.axis_index("row"), lax.axis_index("col")
    scal = jnp.stack([r, c, pivot_blocks[0]]).astype(jnp.int32)
    targets = child_map.reshape(slots)
    stiff = stiff_diag.reshape(order // bs, bs)
    outgoing = child_blocks.reshape(frames, slot_count, bs, bs)
    incoming = lax.all_to_all(outgoing, "front", split_axis=0, concat_axis=0, tiled=True)
    blocks = incoming.reshape(slots, bs, bs)
    smem = pl.BlockSpec(memory_space=pltpu.SMEM)
    vmem = pl.BlockSpec(memory_space=pltpu.VMEM)
    params = pltpu.CompilerParams(vmem_limit_bytes=VMEM_BYTES)
    panel = pl.pallas_call(
        functools.partial(panel_kernel, slots, across),
        out_shape=jax.ShapeDtypeStruct((down, bs, bs), F32),
        in_specs=[smem, vmem],
        out_specs=vmem,
        compiler_params=params,
    )(targets, blocks)
    lead = lax.all_gather(panel[0], ("row", "col"), axis=0, tiled=False)
    piece = panel[1:]
    turned = lax.ppermute(
        piece,
        ("row", "col"),
        [(a * cols_n + b, b * cols_n + a) for a in range(rows_n) for b in range(cols_n)],
    )
    row_part = lax.all_gather(piece, "col", axis=0, tiled=False)
    col_part = lax.all_gather(turned, "row", axis=0, tiled=False)
    n = NP * bs
    inverse, full = pl.pallas_call(
        functools.partial(factor_kernel, bs),
        out_shape=[jax.ShapeDtypeStruct((n, n), F32)] * 2,
        in_specs=[smem, vmem, vmem],
        out_specs=[vmem, vmem],
        scratch_shapes=[pltpu.VMEM((n, 2 * n), F32)],
        compiler_params=params,
        cost_estimate=pl.CostEstimate(
            flops=20_000_000_000, bytes_accessed=4 * 1024 * 1024, transcendentals=0
        ),
    )(scal, lead, stiff[:NP])

    def whole(shape):
        return pl.BlockSpec(shape, lambda i: (0,) * len(shape))

    result = pl.pallas_call(
        functools.partial(update_kernel, slots, across, rows_n, cols_n, bs),
        grid=(down,),
        out_shape=jax.ShapeDtypeStruct((down, bs * across, bs), F32),
        in_specs=[
            smem,
            smem,
            whole(blocks.shape),
            whole(row_part.shape),
            whole(col_part.shape),
            whole((n, n)),
            whole((n, n)),
            whole(stiff.shape),
        ],
        out_specs=pl.BlockSpec((1, bs * across, bs), lambda i: (i, 0, 0)),
        scratch_shapes=[
            pltpu.VMEM((n, n), BF16),
            pltpu.VMEM((n, n), BF16),
            pltpu.VMEM((across * bs, n), BF16),
            pltpu.VMEM((across * bs, n), BF16),
            pltpu.VMEM((across, bs, bs), F32),
        ],
        compiler_params=params,
    )(scal, targets, blocks, row_part, col_part, full, inverse, stiff)
    return result.reshape(1, 1, down, bs, 1, across, bs)


def solution(mesh):
    placed = (
        P("front", "row", "col", None, None, None, None),
        P("front", "row", "col", None, None),
        P("front", None),
        P("front"),
    )
    return jax.shard_map(
        on_device,
        mesh=mesh,
        in_specs=placed,
        out_specs=P("front", "row", None, None, "col", None, None),
        check_vma=False,
    )
```

```python
import functools

import jax
import jax.numpy as jnp
from jax import lax
from jax.experimental import pallas as pl
from jax.experimental.pallas import tpu as pltpu
from jax.sharding import PartitionSpec as P

NP = 4
GROUP = 4
NT = (((1,), (1,)), ((), ()))
TN = (((0,), (0,)), ((), ()))
NN = (((1,), (0,)), ((), ()))
F32 = jnp.float32
BF16 = jnp.bfloat16
VMEM_BYTES = 44 * 1024 * 1024


def exact_dot(a, b, dims):
    return lax.dot_general(
        a, b, dims, precision=lax.Precision.HIGHEST, preferred_element_type=F32
    )


def split(x):
    high = x.astype(BF16)
    return high, (x - high.astype(F32)).astype(BF16)


def split_dot(a, b, dims):
    dot = functools.partial(lax.dot_general, dimension_numbers=dims, preferred_element_type=F32)
    return dot(a[0], b[0]) + (dot(a[0], b[1]) + dot(a[1], b[0]))


def panel_kernel(slots, across, targets, blocks, out):
    out[...] = jnp.zeros_like(out)

    def body(s, carry):
        t = targets[s]

        @pl.when(lax.rem(t, across) == 0)
        def _():
            i = lax.div(t, across)
            out[i] = out[i] + blocks[s]

        return carry

    lax.fori_loop(0, slots, body, 0)


def invert_diagonal(block, bs):
    tiles = bs // 8
    sub = lax.broadcasted_iota(jnp.int32, (8, bs), 0)
    lane = lax.broadcasted_iota(jnp.int32, (8, bs), 1)
    m = [block[8 * i : 8 * i + 8, :] for i in range(tiles)]
    w = [(lane == sub + 8 * i).astype(F32) for i in range(tiles)]
    for k in range(0, bs, GROUP):
        top = k // 8
        cols = [
            {
                i: jnp.broadcast_to(m[i][:, k + t : k + t + 1], (8, bs))
                for i in range(top, tiles)
            }
            for t in range(GROUP)
        ]
        for t in range(GROUP):
            kk = k % 8 + t
            inv = 1.0 / cols[t][top][kk : kk + 1, :]
            q = m[top][kk : kk + 1, :] * inv
            wq = w[top][kk : kk + 1, :] * inv
            rest = {s: cols[s][top][kk : kk + 1, :] * inv for s in range(t + 1, GROUP)}
            for i in range(top, tiles):
                c = cols[t][i]
                if i == top:
                    if kk == 7:
                        continue
                    c = jnp.where(sub > kk, c, 0.0)
                m[i] = m[i] - c * q
                w[i] = w[i] - c * wq
                for s in rest:
                    cols[s][i] = cols[s][i] - c * rest[s]
    out = []
    for i in range(tiles):
        d = jnp.sum(jnp.where(lane == sub + 8 * i, m[i], 0.0), axis=1, keepdims=True)
        out.append(w[i] * lax.rsqrt(d))
    return jnp.concatenate(out, axis=0)


def factor_kernel(bs, scal, lead, stiff, inverse, full, work):
    n = NP * bs
    pivot = scal[2]
    row = lax.broadcasted_iota(jnp.int32, (bs, bs), 0)
    col = lax.broadcasted_iota(jnp.int32, (bs, bs), 1)
    eye = row == col
    for i in range(NP):
        for j in range(i + 1):
            block = lead[i * NP + j]
            if i == j:
                block = jnp.where(row >= col, block, block.T)
                block = block + jnp.where(eye, stiff[i : i + 1, :], 0.0)
            full[i * bs : (i + 1) * bs, j * bs : (j + 1) * bs] = block
            if i != j:
                full[j * bs : (j + 1) * bs, i * bs : (i + 1) * bs] = block.T
    for i in range(NP):
        for j in range(NP):
            ok = jnp.logical_and(i < pivot, j < pivot)
            rest = eye.astype(F32) if i == j else jnp.zeros((bs, bs), F32)
            work[i * bs : (i + 1) * bs, j * bs : (j + 1) * bs] = jnp.where(
                ok, full[i * bs : (i + 1) * bs, j * bs : (j + 1) * bs], rest
            )
            work[i * bs : (i + 1) * bs, n + j * bs : n + (j + 1) * bs] = (
                eye.astype(F32) if i == j else jnp.zeros((bs, bs), F32)
            )

    for b in range(NP):
        lo, hi = b * bs, (b + 1) * bs
        w = invert_diagonal(work[lo:hi, lo:hi], bs)
        done = exact_dot(w, work[lo:hi, lo : n + hi], NN)
        inverse[lo:hi, :] = jnp.where(b < pivot, jnp.concatenate(
            [done[:, n - lo :]] + ([jnp.zeros((bs, n - hi), F32)] if hi < n else []), axis=1
        ), 0.0)
        if hi < n:
            work[hi:, hi : n + hi] = work[hi:, hi : n + hi] - exact_dot(
                done[:, bs : n - lo], done[:, bs:], TN
            )


def update_kernel(
    slots, across, rows_n, cols_n, bs, scal, targets, blocks, row_part, col_part, full, inverse,
    stiff, out, inv_hi, inv_lo, col_hi, col_lo, total,
):
    i = pl.program_id(0)
    down = pl.num_programs(0)
    r, c, pivot = scal[0], scal[1], scal[2]

    def solved(part, k, place, owners):
        def first():
            return full[pl.ds(pl.multiple_of(place * bs, bs), bs), :]

        a = jnp.concatenate([part[owner, jnp.maximum(k - 1, 0)] for owner in owners], axis=1)
        a = jnp.where(k == 0, first(), a)
        return split_dot(split(a), (inv_hi[...], inv_lo[...]), NT)

    @pl.when(i == 0)
    def _():
        high, low = split(inverse[...])
        inv_hi[...] = high
        inv_lo[...] = low

    high, low = split(solved(col_part, i, c, [lax.rem(r - j + rows_n, rows_n) for j in range(NP)]))
    at = pl.ds(pl.multiple_of(i * bs, bs), bs)
    col_hi[at, :] = high
    col_lo[at, :] = low
    x = solved(row_part, i, r, range(NP))
    mine = split(x)
    total[...] = jnp.zeros_like(total)

    def body(s, carry):
        t = targets[s]

        @pl.when(lax.div(t, across) == i)
        def _():
            j = lax.rem(t, across)
            total[j] = total[j] + blocks[s]

        return carry

    lax.fori_loop(0, slots, body, 0)
    place = r + rows_n * i
    row = lax.broadcasted_iota(jnp.int32, (bs, bs), 0)
    col = lax.broadcasted_iota(jnp.int32, (bs, bs), 1)
    stiff_row = stiff[pl.ds(place, 1), :]

    for j in range(across):
        across_place = c + cols_n * j

        @pl.when(place > across_place)
        def _():
            at_j = slice(j * bs, (j + 1) * bs)
            v = total[j] - split_dot(mine, (col_hi[at_j, :], col_lo[at_j, :]), NT)
            total[j] = v

        @pl.when(place == across_place)
        def _():
            at_j = slice(j * bs, (j + 1) * bs)
            v = total[j] - split_dot(mine, (col_hi[at_j, :], col_lo[at_j, :]), NT)
            v = v + jnp.where(row == col, stiff_row, 0.0)
            total[j] = jnp.where(row >= col, v, 0.0)

        if j == 0:
            for b in range(NP):

                @pl.when((c == b) & (b < pivot))
                def _():
                    mask = (place > b) | ((place == b) & (row >= col))
                    total[0] = jnp.where(mask, x[:, b * bs : (b + 1) * bs], 0.0)

        out[0, pl.ds(j, bs, stride=across), :] = total[j]


def on_device(child_blocks, child_map, stiff_diag, pivot_blocks):
    frames, slot_count, bs = child_blocks.shape[3:6]
    rows_n, cols_n = lax.axis_size("row"), lax.axis_size("col")
    order = stiff_diag.shape[1]
    down, across = order // (bs * rows_n), order // (bs * cols_n)
    slots = frames * slot_count
    r, c = lax.axis_index("row"), lax.axis_index("col")
    scal = jnp.stack([r, c, pivot_blocks[0]]).astype(jnp.int32)
    targets = child_map.reshape(slots)
    stiff = stiff_diag.reshape(order // bs, bs)
    outgoing = child_blocks.reshape(frames, slot_count, bs, bs)
    incoming = lax.all_to_all(outgoing, "front", split_axis=0, concat_axis=0, tiled=True)
    blocks = incoming.reshape(slots, bs, bs)
    smem = pl.BlockSpec(memory_space=pltpu.SMEM)
    vmem = pl.BlockSpec(memory_space=pltpu.VMEM)
    params = pltpu.CompilerParams(vmem_limit_bytes=VMEM_BYTES)
    panel = pl.pallas_call(
        functools.partial(panel_kernel, slots, across),
        out_shape=jax.ShapeDtypeStruct((down, bs, bs), F32),
        in_specs=[smem, vmem],
        out_specs=vmem,
        compiler_params=params,
    )(targets, blocks)
    lead = lax.all_gather(panel[0], ("row", "col"), axis=0, tiled=False)
    piece = panel[1:]
    turned = [
        lax.ppermute(
            piece,
            ("row", "col"),
            [
                (a * cols_n + b, (b + k) % rows_n * cols_n + a)
                for a in range(rows_n)
                for b in range(cols_n)
            ],
        )
        for k in range(NP)
    ]
    row_part = lax.all_gather(piece, "col", axis=0, tiled=False)
    col_part = jnp.stack(turned)
    n = NP * bs
    inverse, full = pl.pallas_call(
        functools.partial(factor_kernel, bs),
        out_shape=[jax.ShapeDtypeStruct((n, n), F32)] * 2,
        in_specs=[smem, vmem, vmem],
        out_specs=[vmem, vmem],
        scratch_shapes=[pltpu.VMEM((n, 2 * n), F32)],
        compiler_params=params,
        cost_estimate=pl.CostEstimate(
            flops=20_000_000_000, bytes_accessed=4 * 1024 * 1024, transcendentals=0
        ),
    )(scal, lead, stiff[:NP])

    def whole(shape):
        return pl.BlockSpec(shape, lambda i: (0,) * len(shape))

    result = pl.pallas_call(
        functools.partial(update_kernel, slots, across, rows_n, cols_n, bs),
        grid=(down,),
        out_shape=jax.ShapeDtypeStruct((down, bs * across, bs), F32),
        in_specs=[
            smem,
            smem,
            whole(blocks.shape),
            whole(row_part.shape),
            whole(col_part.shape),
            whole((n, n)),
            whole((n, n)),
            whole(stiff.shape),
        ],
        out_specs=pl.BlockSpec((1, bs * across, bs), lambda i: (i, 0, 0)),
        scratch_shapes=[
            pltpu.VMEM((n, n), BF16),
            pltpu.VMEM((n, n), BF16),
            pltpu.VMEM((across * bs, n), BF16),
            pltpu.VMEM((across * bs, n), BF16),
            pltpu.VMEM((across, bs, bs), F32),
        ],
        compiler_params=params,
    )(scal, targets, blocks, row_part, col_part, full, inverse, stiff)
    return result.reshape(1, 1, down, bs, 1, across, bs)


def solution(mesh):
    placed = (
        P("front", "row", "col", None, None, None, None),
        P("front", "row", "col", None, None),
        P("front", None),
        P("front"),
    )
    return jax.shard_map(
        on_device,
        mesh=mesh,
        in_specs=placed,
        out_specs=P("front", "row", None, None, "col", None, None),
        check_vma=False,
    )
```

```python
import functools

import jax
import jax.numpy as jnp
from jax import lax
from jax.experimental import pallas as pl
from jax.experimental.pallas import tpu as pltpu
from jax.sharding import PartitionSpec as P

NP = 4
GROUP = 4
NT = (((1,), (1,)), ((), ()))
TN = (((0,), (0,)), ((), ()))
NN = (((1,), (0,)), ((), ()))
F32 = jnp.float32
BF16 = jnp.bfloat16
VMEM_BYTES = 44 * 1024 * 1024


def exact_dot(a, b, dims):
    return lax.dot_general(
        a, b, dims, precision=lax.Precision.HIGHEST, preferred_element_type=F32
    )


def split(x):
    high = x.astype(BF16)
    return high, (x - high.astype(F32)).astype(BF16)


def split_dot(a, b, dims):
    dot = functools.partial(lax.dot_general, dimension_numbers=dims, preferred_element_type=F32)
    return dot(a[0], b[0]) + (dot(a[0], b[1]) + dot(a[1], b[0]))


def panel_kernel(slots, across, targets, blocks, out):
    out[...] = jnp.zeros_like(out)

    def body(s, carry):
        t = targets[s]

        @pl.when(lax.rem(t, across) == 0)
        def _():
            i = lax.div(t, across)
            out[i] = out[i] + blocks[s]

        return carry

    lax.fori_loop(0, slots, body, 0)


def lead_kernel(rows_n, cols_n, src, out, got, send, recv):
    r, c = lax.axis_index("row"), lax.axis_index("col")
    sibling = c + 1 - 2 * lax.rem(c, 2)
    mate = lax.rem(c + 2, cols_n)
    others = [{"row": lax.rem(r + d, rows_n)} for d in range(1, rows_n)]
    barrier = pltpu.get_barrier_semaphore()
    for device in others + [{"col": sibling}, {"col": mate}]:
        pl.semaphore_signal(barrier, inc=1, device_id=device, device_id_type=pl.DeviceIdType.MESH)
    got[c, r] = src[...]
    pl.semaphore_wait(barrier, rows_n + 1)

    def copy(column, place, device, at):
        block = got.at[column, place]
        return pltpu.make_async_remote_copy(
            src_ref=block,
            dst_ref=block,
            send_sem=send.at[at],
            recv_sem=recv.at[at],
            device_id=device,
            device_id_type=pl.DeviceIdType.MESH,
        )

    down = [copy(c, r, device, d) for d, device in enumerate(others)]
    for one in down:
        one.start()
    base = rows_n - 1
    near, far, passed = [], [], []
    for d in range(rows_n):
        place = lax.rem(r - d + rows_n, rows_n)
        if d:
            down[d - 1].wait_recv()
        far.append(copy(c, place, {"col": mate}, base + d))
        near.append(copy(c, place, {"col": sibling}, base + rows_n + d))
        far[-1].start()
        near[-1].start()
    for d in range(rows_n):
        place = lax.rem(r - d + rows_n, rows_n)
        far[d].wait_recv()
        passed.append(copy(mate, place, {"col": sibling}, base + 2 * rows_n + d))
        passed[-1].start()
    for one in near + passed:
        one.wait_recv()
    for one in down + far + near + passed:
        one.wait_send()
    for j in range(cols_n):
        for i in range(rows_n):
            out[j * rows_n + i] = got[j, i]


def invert_diagonal(block, bs):
    tiles = bs // 8
    sub = lax.broadcasted_iota(jnp.int32, (8, bs), 0)
    lane = lax.broadcasted_iota(jnp.int32, (8, bs), 1)
    m = [block[8 * i : 8 * i + 8, :] for i in range(tiles)]
    w = [(lane == sub + 8 * i).astype(F32) for i in range(tiles)]
    for k in range(0, bs, GROUP):
        top = k // 8
        cols = [
            {
                i: jnp.broadcast_to(m[i][:, k + t : k + t + 1], (8, bs))
                for i in range(top, tiles)
            }
            for t in range(GROUP)
        ]
        for t in range(GROUP):
            kk = k % 8 + t
            inv = 1.0 / cols[t][top][kk : kk + 1, :]
            q = m[top][kk : kk + 1, :] * inv
            wq = w[top][kk : kk + 1, :] * inv
            rest = {s: cols[s][top][kk : kk + 1, :] * inv for s in range(t + 1, GROUP)}
            for i in range(top, tiles):
                c = cols[t][i]
                if i == top:
                    if kk == 7:
                        continue
                    c = jnp.where(sub > kk, c, 0.0)
                m[i] = m[i] - c * q
                w[i] = w[i] - c * wq
                for s in rest:
                    cols[s][i] = cols[s][i] - c * rest[s]
    out = []
    for i in range(tiles):
        d = jnp.sum(jnp.where(lane == sub + 8 * i, m[i], 0.0), axis=1, keepdims=True)
        out.append(w[i] * lax.rsqrt(d))
    return jnp.concatenate(out, axis=0)


def factor_kernel(bs, scal, lead, stiff, inverse, full, work):
    n = NP * bs
    pivot = scal[2]
    row = lax.broadcasted_iota(jnp.int32, (bs, bs), 0)
    col = lax.broadcasted_iota(jnp.int32, (bs, bs), 1)
    eye = row == col
    for i in range(NP):
        for j in range(i + 1):
            block = lead[j * NP + i]
            if i == j:
                block = jnp.where(row >= col, block, block.T)
                block = block + jnp.where(eye, stiff[i : i + 1, :], 0.0)
            full[i * bs : (i + 1) * bs, j * bs : (j + 1) * bs] = block
            if i != j:
                full[j * bs : (j + 1) * bs, i * bs : (i + 1) * bs] = block.T
    for i in range(NP):
        for j in range(NP):
            ok = jnp.logical_and(i < pivot, j < pivot)
            rest = eye.astype(F32) if i == j else jnp.zeros((bs, bs), F32)
            work[i * bs : (i + 1) * bs, j * bs : (j + 1) * bs] = jnp.where(
                ok, full[i * bs : (i + 1) * bs, j * bs : (j + 1) * bs], rest
            )
            work[i * bs : (i + 1) * bs, n + j * bs : n + (j + 1) * bs] = (
                eye.astype(F32) if i == j else jnp.zeros((bs, bs), F32)
            )

    for b in range(NP):
        lo, hi = b * bs, (b + 1) * bs
        w = invert_diagonal(work[lo:hi, lo:hi], bs)
        done = exact_dot(w, work[lo:hi, lo : n + hi], NN)
        inverse[lo:hi, :] = jnp.where(b < pivot, jnp.concatenate(
            [done[:, n - lo :]] + ([jnp.zeros((bs, n - hi), F32)] if hi < n else []), axis=1
        ), 0.0)
        if hi < n:
            work[hi:, hi : n + hi] = work[hi:, hi : n + hi] - exact_dot(
                done[:, bs : n - lo], done[:, bs:], TN
            )


def update_kernel(
    slots, across, rows_n, cols_n, bs, scal, targets, blocks, row_part, col_part, full, inverse,
    stiff, out, row_x, col_hi, col_lo, total,
):
    i = pl.program_id(0)
    down = row_part.shape[1] + 1
    r, c, pivot = scal[0], scal[1], scal[2]

    def solved(part, place, owners, inv):
        first = full[pl.ds(pl.multiple_of(place * bs, bs), bs), :]
        rest = jnp.concatenate(
            [part[owner].reshape((down - 1) * bs, bs) for owner in owners], axis=1
        )
        return split_dot(split(jnp.concatenate([first, rest], axis=0)), inv, NT)

    @pl.when(i == 0)
    def _():
        inv = split(inverse[...])
        high, low = split(
            solved(col_part, c, [lax.rem(r - j + rows_n, rows_n) for j in range(NP)], inv)
        )
        col_hi[...] = high
        col_lo[...] = low
        row_x[...] = solved(row_part, r, range(NP), inv)

    x = row_x[pl.ds(pl.multiple_of(i * bs, bs), bs), :]
    mine = split(x)
    total[...] = jnp.zeros_like(total)

    def body(s, carry):
        t = targets[s]

        @pl.when(lax.div(t, across) == i)
        def _():
            j = lax.rem(t, across)
            total[j] = total[j] + blocks[s]

        return carry

    lax.fori_loop(0, slots, body, 0)
    place = r + rows_n * i
    row = lax.broadcasted_iota(jnp.int32, (bs, bs), 0)
    col = lax.broadcasted_iota(jnp.int32, (bs, bs), 1)
    stiff_row = stiff[pl.ds(place, 1), :]

    for j in range(across):
        across_place = c + cols_n * j

        @pl.when(place > across_place)
        def _():
            at_j = slice(j * bs, (j + 1) * bs)
            v = total[j] - split_dot(mine, (col_hi[at_j, :], col_lo[at_j, :]), NT)
            total[j] = v

        @pl.when(place == across_place)
        def _():
            at_j = slice(j * bs, (j + 1) * bs)
            v = total[j] - split_dot(mine, (col_hi[at_j, :], col_lo[at_j, :]), NT)
            v = v + jnp.where(row == col, stiff_row, 0.0)
            total[j] = jnp.where(row >= col, v, 0.0)

        if j == 0:
            for b in range(NP):

                @pl.when((c == b) & (b < pivot))
                def _():
                    mask = (place > b) | ((place == b) & (row >= col))
                    total[0] = jnp.where(mask, x[:, b * bs : (b + 1) * bs], 0.0)

        out[0, pl.ds(j, bs, stride=across), :] = total[j]


def on_device(child_blocks, child_map, stiff_diag, pivot_blocks):
    frames, slot_count, bs = child_blocks.shape[3:6]
    rows_n, cols_n = lax.axis_size("row"), lax.axis_size("col")
    order = stiff_diag.shape[1]
    down, across = order // (bs * rows_n), order // (bs * cols_n)
    slots = frames * slot_count
    r, c = lax.axis_index("row"), lax.axis_index("col")
    scal = jnp.stack([r, c, pivot_blocks[0]]).astype(jnp.int32)
    targets = child_map.reshape(slots)
    stiff = stiff_diag.reshape(order // bs, bs)
    outgoing = child_blocks.reshape(frames, slot_count, bs, bs)
    incoming = lax.all_to_all(outgoing, "front", split_axis=0, concat_axis=0, tiled=True)
    blocks = incoming.reshape(slots, bs, bs)
    smem = pl.BlockSpec(memory_space=pltpu.SMEM)
    vmem = pl.BlockSpec(memory_space=pltpu.VMEM)
    params = pltpu.CompilerParams(vmem_limit_bytes=VMEM_BYTES)
    panel = pl.pallas_call(
        functools.partial(panel_kernel, slots, across),
        out_shape=jax.ShapeDtypeStruct((down, bs, bs), F32),
        in_specs=[smem, vmem],
        out_specs=vmem,
        compiler_params=params,
    )(targets, blocks)
    copies = 4 * rows_n - 1
    lead = pl.pallas_call(
        functools.partial(lead_kernel, rows_n, cols_n),
        out_shape=jax.ShapeDtypeStruct((cols_n * rows_n, bs, bs), F32),
        in_specs=[vmem],
        out_specs=vmem,
        scratch_shapes=[
            pltpu.VMEM((cols_n, rows_n, bs, bs), F32),
            pltpu.SemaphoreType.DMA((copies,)),
            pltpu.SemaphoreType.DMA((copies,)),
        ],
        compiler_params=pltpu.CompilerParams(collective_id=0, has_side_effects=True),
    )(panel[0])
    piece = panel[1:]
    later, lead = lax.optimization_barrier((piece, lead))
    turned = [
        lax.ppermute(
            piece if k < 2 else later,
            ("row", "col"),
            [
                (a * cols_n + b, (b + k) % rows_n * cols_n + a)
                for a in range(rows_n)
                for b in range(cols_n)
            ],
        )
        for k in range(NP)
    ]
    row_part = lax.all_gather(piece, "col", axis=0, tiled=False)
    col_part = jnp.stack(turned)
    n = NP * bs
    inverse, full = pl.pallas_call(
        functools.partial(factor_kernel, bs),
        out_shape=[jax.ShapeDtypeStruct((n, n), F32)] * 2,
        in_specs=[smem, vmem, vmem],
        out_specs=[vmem, vmem],
        scratch_shapes=[pltpu.VMEM((n, 2 * n), F32)],
        compiler_params=params,
        cost_estimate=pl.CostEstimate(
            flops=20_000_000_000, bytes_accessed=4 * 1024 * 1024, transcendentals=0
        ),
    )(scal, lead, stiff[:NP])

    def whole(shape):
        return pl.BlockSpec(shape, lambda i: (0,) * len(shape))

    result = pl.pallas_call(
        functools.partial(update_kernel, slots, across, rows_n, cols_n, bs),
        grid=(down,),
        out_shape=jax.ShapeDtypeStruct((down, bs * across, bs), F32),
        in_specs=[
            smem,
            smem,
            whole(blocks.shape),
            whole(row_part.shape),
            whole(col_part.shape),
            whole((n, n)),
            whole((n, n)),
            whole(stiff.shape),
        ],
        out_specs=pl.BlockSpec((1, bs * across, bs), lambda i: (i, 0, 0)),
        scratch_shapes=[
            pltpu.VMEM((down * bs, n), F32),
            pltpu.VMEM((across * bs, n), BF16),
            pltpu.VMEM((across * bs, n), BF16),
            pltpu.VMEM((across, bs, bs), F32),
        ],
        compiler_params=params,
    )(scal, targets, blocks, row_part, col_part, full, inverse, stiff)
    return result.reshape(1, 1, down, bs, 1, across, bs)


def solution(mesh):
    placed = (
        P("front", "row", "col", None, None, None, None),
        P("front", "row", "col", None, None),
        P("front", None),
        P("front"),
    )
    return jax.shard_map(
        on_device,
        mesh=mesh,
        in_specs=placed,
        out_specs=P("front", "row", None, None, "col", None, None),
        check_vma=False,
    )
```

```python
import functools

import jax
import jax.numpy as jnp
from jax import lax
from jax.experimental import pallas as pl
from jax.experimental.pallas import tpu as pltpu
from jax.sharding import PartitionSpec as P

NP = 4
GROUP = 4
NT = (((1,), (1,)), ((), ()))
TN = (((0,), (0,)), ((), ()))
NN = (((1,), (0,)), ((), ()))
F32 = jnp.float32
BF16 = jnp.bfloat16
VMEM_BYTES = 44 * 1024 * 1024


def exact_dot(a, b, dims):
    return lax.dot_general(
        a, b, dims, precision=lax.Precision.HIGHEST, preferred_element_type=F32
    )


def split(x):
    high = x.astype(BF16)
    return high, (x - high.astype(F32)).astype(BF16)


def split_dot(a, b, dims):
    dot = functools.partial(lax.dot_general, dimension_numbers=dims, preferred_element_type=F32)
    return dot(a[0], b[0]) + (dot(a[0], b[1]) + dot(a[1], b[0]))


def panel_kernel(slots, across, targets, blocks, out):
    out[...] = jnp.zeros_like(out)

    def body(s, carry):
        t = targets[s]

        @pl.when(lax.rem(t, across) == 0)
        def _():
            i = lax.div(t, across)
            out[i] = out[i] + blocks[s]

        return carry

    lax.fori_loop(0, slots, body, 0)


def lead_kernel(rows_n, cols_n, src, out, got, send, recv):
    r, c = lax.axis_index("row"), lax.axis_index("col")
    sibling = c + 1 - 2 * lax.rem(c, 2)
    mate = lax.rem(c + 2, cols_n)
    others = [{"row": lax.rem(r + d, rows_n)} for d in range(1, rows_n)]
    barrier = pltpu.get_barrier_semaphore()
    for device in others + [{"col": sibling}, {"col": mate}]:
        pl.semaphore_signal(barrier, inc=1, device_id=device, device_id_type=pl.DeviceIdType.MESH)
    got[c, r] = src[...]
    pl.semaphore_wait(barrier, rows_n + 1)

    def copy(column, place, device, at):
        block = got.at[column, place]
        return pltpu.make_async_remote_copy(
            src_ref=block,
            dst_ref=block,
            send_sem=send.at[at],
            recv_sem=recv.at[at],
            device_id=device,
            device_id_type=pl.DeviceIdType.MESH,
        )

    down = [copy(c, r, device, d) for d, device in enumerate(others)]
    for one in down:
        one.start()
    base = rows_n - 1
    near, far, passed = [], [], []
    for d in range(rows_n):
        place = lax.rem(r - d + rows_n, rows_n)
        if d:
            down[d - 1].wait_recv()
        far.append(copy(c, place, {"col": mate}, base + d))
        near.append(copy(c, place, {"col": sibling}, base + rows_n + d))
        far[-1].start()
        near[-1].start()
    for d in range(rows_n):
        place = lax.rem(r - d + rows_n, rows_n)
        far[d].wait_recv()
        passed.append(copy(mate, place, {"col": sibling}, base + 2 * rows_n + d))
        passed[-1].start()
    for one in near + passed:
        one.wait_recv()
    for one in down + far + near + passed:
        one.wait_send()
    for j in range(cols_n):
        for i in range(rows_n):
            out[j * rows_n + i] = got[j, i]


def invert_diagonal(block, bs):
    tiles = bs // 8
    sub = lax.broadcasted_iota(jnp.int32, (8, bs), 0)
    lane = lax.broadcasted_iota(jnp.int32, (8, bs), 1)
    m = [block[8 * i : 8 * i + 8, :] for i in range(tiles)]
    w = [(lane == sub + 8 * i).astype(F32) for i in range(tiles)]
    for k in range(0, bs, GROUP):
        top = k // 8
        cols = [
            {
                i: jnp.broadcast_to(m[i][:, k + t : k + t + 1], (8, bs))
                for i in range(top, tiles)
            }
            for t in range(GROUP)
        ]
        for t in range(GROUP):
            kk = k % 8 + t
            inv = 1.0 / cols[t][top][kk : kk + 1, :]
            q = m[top][kk : kk + 1, :] * inv
            wq = w[top][kk : kk + 1, :] * inv
            rest = {s: cols[s][top][kk : kk + 1, :] * inv for s in range(t + 1, GROUP)}
            for i in range(top, tiles):
                c = cols[t][i]
                if i == top:
                    if kk == 7:
                        continue
                    c = jnp.where(sub > kk, c, 0.0)
                m[i] = m[i] - c * q
                w[i] = w[i] - c * wq
                for s in rest:
                    cols[s][i] = cols[s][i] - c * rest[s]
    out = []
    for i in range(tiles):
        d = jnp.sum(jnp.where(lane == sub + 8 * i, m[i], 0.0), axis=1, keepdims=True)
        out.append(w[i] * lax.rsqrt(d))
    return jnp.concatenate(out, axis=0)


def factor_kernel(bs, scal, lead, stiff, inverse, full, work):
    n = NP * bs
    pivot = scal[2]
    row = lax.broadcasted_iota(jnp.int32, (bs, bs), 0)
    col = lax.broadcasted_iota(jnp.int32, (bs, bs), 1)
    eye = row == col
    for i in range(NP):
        for j in range(i + 1):
            block = lead[j * NP + i]
            if i == j:
                block = jnp.where(row >= col, block, block.T)
                block = block + jnp.where(eye, stiff[i : i + 1, :], 0.0)
            full[i * bs : (i + 1) * bs, j * bs : (j + 1) * bs] = block
            if i != j:
                full[j * bs : (j + 1) * bs, i * bs : (i + 1) * bs] = block.T
    for i in range(NP):
        for j in range(NP):
            ok = jnp.logical_and(i < pivot, j < pivot)
            rest = eye.astype(F32) if i == j else jnp.zeros((bs, bs), F32)
            work[i * bs : (i + 1) * bs, j * bs : (j + 1) * bs] = jnp.where(
                ok, full[i * bs : (i + 1) * bs, j * bs : (j + 1) * bs], rest
            )
            work[i * bs : (i + 1) * bs, n + j * bs : n + (j + 1) * bs] = (
                eye.astype(F32) if i == j else jnp.zeros((bs, bs), F32)
            )

    for b in range(NP):
        lo, hi = b * bs, (b + 1) * bs
        w = invert_diagonal(work[lo:hi, lo:hi], bs)
        done = exact_dot(w, work[lo:hi, lo : n + hi], NN)
        inverse[lo:hi, :] = jnp.where(b < pivot, jnp.concatenate(
            [done[:, n - lo :]] + ([jnp.zeros((bs, n - hi), F32)] if hi < n else []), axis=1
        ), 0.0)
        if hi < n:
            work[hi:, hi : n + hi] = work[hi:, hi : n + hi] - exact_dot(
                done[:, bs : n - lo], done[:, bs:], TN
            )


def update_kernel(
    slots, across, rows_n, cols_n, bs, scal, targets, blocks, row_part, col_0, col_1, col_2, col_3,
    full, inverse, stiff, out, row_x, col_hi, col_lo, total,
):
    i = pl.program_id(0)
    down = row_part.shape[1] + 1
    r, c, pivot = scal[0], scal[1], scal[2]

    @pl.when(i == 0)
    def _():
        inv = split(inverse[...])
        row_x[0:bs, :] = full[pl.ds(pl.multiple_of(c * bs, bs), bs), :]
        for k, part in enumerate((col_0, col_1, col_2, col_3)):
            owner = lax.rem(r - k + rows_n, rows_n)
            at = pl.ds(pl.multiple_of(owner * bs, bs), bs)
            row_x[bs : down * bs, at] = part[...].reshape((down - 1) * bs, bs)
        high, low = split(split_dot(split(row_x[...]), inv, NT))
        col_hi[...] = high
        col_lo[...] = low
        first = full[pl.ds(pl.multiple_of(r * bs, bs), bs), :]
        rest = jnp.concatenate(
            [row_part[j].reshape((down - 1) * bs, bs) for j in range(NP)], axis=1
        )
        row_x[...] = split_dot(split(jnp.concatenate([first, rest], axis=0)), inv, NT)

    x = row_x[pl.ds(pl.multiple_of(i * bs, bs), bs), :]
    mine = split(x)
    total[...] = jnp.zeros_like(total)

    def body(s, carry):
        t = targets[s]

        @pl.when(lax.div(t, across) == i)
        def _():
            j = lax.rem(t, across)
            total[j] = total[j] + blocks[s]

        return carry

    lax.fori_loop(0, slots, body, 0)
    place = r + rows_n * i
    row = lax.broadcasted_iota(jnp.int32, (bs, bs), 0)
    col = lax.broadcasted_iota(jnp.int32, (bs, bs), 1)
    stiff_row = stiff[pl.ds(place, 1), :]

    for j in range(across):
        across_place = c + cols_n * j

        @pl.when(place > across_place)
        def _():
            at_j = slice(j * bs, (j + 1) * bs)
            v = total[j] - split_dot(mine, (col_hi[at_j, :], col_lo[at_j, :]), NT)
            total[j] = v

        @pl.when(place == across_place)
        def _():
            at_j = slice(j * bs, (j + 1) * bs)
            v = total[j] - split_dot(mine, (col_hi[at_j, :], col_lo[at_j, :]), NT)
            v = v + jnp.where(row == col, stiff_row, 0.0)
            total[j] = jnp.where(row >= col, v, 0.0)

        if j == 0:
            for b in range(NP):

                @pl.when((c == b) & (b < pivot))
                def _():
                    mask = (place > b) | ((place == b) & (row >= col))
                    total[0] = jnp.where(mask, x[:, b * bs : (b + 1) * bs], 0.0)

        out[0, pl.ds(j, bs, stride=across), :] = total[j]


def on_device(child_blocks, child_map, stiff_diag, pivot_blocks):
    frames, slot_count, bs = child_blocks.shape[3:6]
    rows_n, cols_n = lax.axis_size("row"), lax.axis_size("col")
    order = stiff_diag.shape[1]
    down, across = order // (bs * rows_n), order // (bs * cols_n)
    slots = frames * slot_count
    r, c = lax.axis_index("row"), lax.axis_index("col")
    scal = jnp.stack([r, c, pivot_blocks[0]]).astype(jnp.int32)
    targets = child_map.reshape(slots)
    stiff = stiff_diag.reshape(order // bs, bs)
    outgoing = child_blocks.reshape(frames, slot_count, bs, bs)
    incoming = lax.all_to_all(outgoing, "front", split_axis=0, concat_axis=0, tiled=True)
    blocks = incoming.reshape(slots, bs, bs)
    smem = pl.BlockSpec(memory_space=pltpu.SMEM)
    vmem = pl.BlockSpec(memory_space=pltpu.VMEM)
    params = pltpu.CompilerParams(vmem_limit_bytes=VMEM_BYTES)
    panel = pl.pallas_call(
        functools.partial(panel_kernel, slots, across),
        out_shape=jax.ShapeDtypeStruct((down, bs, bs), F32),
        in_specs=[smem, vmem],
        out_specs=vmem,
        compiler_params=params,
    )(targets, blocks)
    copies = 4 * rows_n - 1
    lead = pl.pallas_call(
        functools.partial(lead_kernel, rows_n, cols_n),
        out_shape=jax.ShapeDtypeStruct((cols_n * rows_n, bs, bs), F32),
        in_specs=[vmem],
        out_specs=vmem,
        scratch_shapes=[
            pltpu.VMEM((cols_n, rows_n, bs, bs), F32),
            pltpu.SemaphoreType.DMA((copies,)),
            pltpu.SemaphoreType.DMA((copies,)),
        ],
        compiler_params=pltpu.CompilerParams(collective_id=0, has_side_effects=True),
    )(panel[0])
    piece = panel[1:]
    piece, lead = lax.optimization_barrier((piece, lead))
    turned = [
        lax.ppermute(
            piece,
            ("row", "col"),
            [
                (a * cols_n + b, (b + k) % rows_n * cols_n + a)
                for a in range(rows_n)
                for b in range(cols_n)
            ],
        )
        for k in range(NP)
    ]
    row_part = lax.all_gather(piece, "col", axis=0, tiled=False)
    n = NP * bs
    inverse, full = pl.pallas_call(
        functools.partial(factor_kernel, bs),
        out_shape=[jax.ShapeDtypeStruct((n, n), F32)] * 2,
        in_specs=[smem, vmem, vmem],
        out_specs=[vmem, vmem],
        scratch_shapes=[pltpu.VMEM((n, 2 * n), F32)],
        compiler_params=params,
        cost_estimate=pl.CostEstimate(
            flops=20_000_000_000, bytes_accessed=4 * 1024 * 1024, transcendentals=0
        ),
    )(scal, lead, stiff[:NP])

    def whole(shape):
        return pl.BlockSpec(shape, lambda i: (0,) * len(shape))

    result = pl.pallas_call(
        functools.partial(update_kernel, slots, across, rows_n, cols_n, bs),
        grid=(down,),
        out_shape=jax.ShapeDtypeStruct((down, bs * across, bs), F32),
        in_specs=[
            smem,
            smem,
            whole(blocks.shape),
            whole(row_part.shape),
            *[whole(piece.shape)] * NP,
            whole((n, n)),
            whole((n, n)),
            whole(stiff.shape),
        ],
        out_specs=pl.BlockSpec((1, bs * across, bs), lambda i: (i, 0, 0)),
        scratch_shapes=[
            pltpu.VMEM((down * bs, n), F32),
            pltpu.VMEM((across * bs, n), BF16),
            pltpu.VMEM((across * bs, n), BF16),
            pltpu.VMEM((across, bs, bs), F32),
        ],
        compiler_params=params,
    )(scal, targets, blocks, row_part, *turned, full, inverse, stiff)
    return result.reshape(1, 1, down, bs, 1, across, bs)


def solution(mesh):
    placed = (
        P("front", "row", "col", None, None, None, None),
        P("front", "row", "col", None, None),
        P("front", None),
        P("front"),
    )
    return jax.shard_map(
        on_device,
        mesh=mesh,
        in_specs=placed,
        out_specs=P("front", "row", None, None, "col", None, None),
        check_vma=False,
    )
```
